32 devices in a mesh: ctx: 4 (over x, core), ch: 8 (over z, y).
Axes of the slice: x: 2, y: 2, z: 4, core: 2. Of those that a mesh axis runs over, the one named last changes fastest.
Arguments:
- streams: bfloat16 [3, 4608, 1024], P(None, 'ch', 'ctx'), may hold values from -6 to 6
- short_taps: float32 [3, 4608, 3], P(None, 'ch'), may hold values from -1 to 1
- filter_in: float32 [32, 64], replicated, may hold values from -1 to 1
- filter_mid: float32 [64, 64], replicated, may hold values from -0.75 to 0.75
- filter_out: float32 [64, 4608], P(None, 'ch'), may hold values from -2 to 2
- decay_rate: float32 [4608], P('ch'), as said below
- skip_gain: float32 [4608], P('ch'), may hold values from 0.5 to 1.5
- out_weight: bfloat16 [4608, 4608], P('ch'), may hold values from -0.09375 to 0.09375
- grad_out: bfloat16 [4608, 1024], P('ch', 'ctx'), may hold values from -6 to 6
Outputs:
- layer_out: bfloat16 [4608, 1024], P('ch', 'ctx')
- grad_streams: bfloat16 [3, 4608, 1024], P(None, 'ch', 'ctx')
- grad_filter_in: float32 [32, 64], replicated
- grad_filter_mid: float32 [64, 64], replicated
- grad_filter_out: float32 [64, 4608], P(None, 'ch')
- grad_out_weight: float32 [4608, 4608], P('ch')
The draws below stay inside these ranges and needn't reach their ends.
Inputs may be any that keep to these rules, and one draw needn't show every extreme that they name: `decay_rate`: every channel's rate lies between 1 / 5120 and 1 / 30.
All inputs are finite; a program needn't handle non-finite values.
Results may differ from the reference program's by a relative error of at most 0.014.
Values may be sent and summed in bfloat16 or wider, within the bound.
A program may use at most 128 MiB of HBM per device.

```python
import math
import jax
import jax.numpy as jnp
from jax import lax

CH = 4608
FH = 64
BANDS = 16
SHORT = 3
SEQ = 1024


def draw_decay_rate(key, part):
    pick_key, level_key = jax.random.split(jax.random.fold_in(key, 17))
    share = 0.5
    slower = jax.random.uniform(pick_key, (CH,)) < share
    lowest = jnp.where(slower, math.log(0.2), math.log(2.0))
    highest = jnp.where(slower, math.log(2.0), math.log(SEQ / 30.0))
    unit = jax.random.uniform(level_key, (CH,))
    return (jnp.exp(lowest + unit * (highest - lowest)) / SEQ).astype(jnp.float32)


def levels(rng, shape, cuts, least, top_value):
    level = 1.0
    for dim, shards_of in cuts:
        steps = jax.random.uniform(jax.random.fold_in(jax.random.fold_in(rng, 6), dim), (shards_of,), jnp.float32, least / len(cuts), top_value / len(cuts))
        level = level * jnp.repeat(jnp.exp(steps), shape[dim] // shards_of).reshape((-1,) + (1,) * (len(shape) - 1 - dim))
    return level


def gaussian(key, dims, spread, bound, cuts=(), kind=jnp.bfloat16):
    factor_of = levels(key, dims, cuts, -0.22, 0.18) if cuts else 1.0
    entries = jax.random.normal(key, dims, jnp.float32) * spread * factor_of
    return jnp.minimum(jnp.maximum(entries, -bound), bound).astype(kind)


def setup_inputs(seed: int = 0) -> dict:
    splits = jax.random.split(jax.random.key(seed), 10)
    return {
        "streams": gaussian(splits[0], (3, CH, SEQ), 1.0, 6.0, ((1, 8), (2, 4))),
        "short_taps": jnp.clip(jax.random.uniform(splits[1], (3, CH, SHORT), jnp.float32, -1.0, 1.0) * levels(splits[1], (3, CH, SHORT), ((1, 8),), -0.4, 0.0), -1.0, 1.0),
        "filter_in": gaussian(splits[2], (2 * BANDS, FH), (2 * BANDS) ** -0.5, 1.0, (), jnp.float32),
        "filter_mid": gaussian(splits[3], (FH, FH), FH ** -0.5, 0.75, (), jnp.float32),
        "filter_out": gaussian(splits[4], (FH, CH), (FH // 8) ** -0.5, 2.0, ((1, 8),), jnp.float32),
        "decay_rate": draw_decay_rate(jax.random.fold_in(splits[9], 71), 0),
        "skip_gain": jnp.clip(0.5 + 1.0 * jax.random.uniform(splits[6], (CH,), jnp.float32) ** levels(splits[6], (CH,), ((0, 8),), -0.2, 0.2), 0.5, 1.5),
        "out_weight": gaussian(splits[7], (CH, CH), CH ** -0.5, 0.09375, ((0, 8),)),
        "grad_out": gaussian(splits[8], (CH, SEQ), 1.0, 6.0, ((0, 8), (1, 4))),
    }


precise = lax.Precision.HIGHEST

def filter_values(filter_in, filter_mid, filter_out, decay_rate, length):
    band_count = filter_in.shape[0] // 2
    lag_index = jnp.arange(length).astype(jnp.int32)
    level_index = jnp.arange(1, band_count + 1).astype(jnp.int32)
    wrapped = level_index[:, None] * lag_index[None, :] % length
    phases = 2.0 * math.pi / length * wrapped.astype(jnp.float32)
    features = jnp.concatenate([jnp.cos(phases), jnp.sin(phases)], axis=0)
    hidden_one = jnp.sin(jnp.einsum('fh,fs->hs', filter_in, features, precision=precise))
    hidden_two = jnp.sin(jnp.einsum('gh,gs->hs', filter_mid, hidden_one, precision=precise))
    raw_out = jnp.einsum('hc,hs->cs', filter_out, hidden_two, precision=precise)
    lag_axis = lag_index.astype(jnp.float32)
    return raw_out * jnp.exp(-decay_rate[:, None] * lag_axis[None, :]) * jnp.sqrt(decay_rate)[:, None]

def short_apply(signal, short_taps):
    taps_width = short_taps.shape[2]
    length = signal.shape[2]
    padded = jnp.pad(signal.astype(jnp.float32), ((0, 0), (0, 0), (taps_width - 1, 0)))
    result = jnp.zeros(signal.shape, jnp.float32)
    for lag_step in range(taps_width):
        begin = taps_width - 1 - lag_step
        result = result + short_taps[:, :, lag_step:lag_step + 1] * padded[:, :, begin:begin + length]
    return result

def short_adjoint(signal, short_taps):
    taps_width = short_taps.shape[2]
    length = signal.shape[2]
    padded = jnp.pad(signal, ((0, 0), (0, 0), (0, taps_width - 1)))
    result = jnp.zeros(signal.shape, signal.dtype)
    for lag_step in range(taps_width):
        result = result + short_taps[:, :, lag_step:lag_step + 1] * padded[:, :, lag_step:lag_step + length]
    return result

def causal_apply(long_filter, signal):
    length = signal.shape[-1]
    spectrum = jnp.fft.rfft(long_filter, 2 * length) * jnp.fft.rfft(signal, 2 * length)
    return jnp.fft.irfft(spectrum, 2 * length)[..., :length]

def correlate(grad_signal, signal):
    length = signal.shape[-1]
    spectrum = jnp.fft.rfft(grad_signal, 2 * length) * jnp.conj(jnp.fft.rfft(signal, 2 * length))
    return jnp.fft.irfft(spectrum, 2 * length)[..., :length]

def reference(streams, short_taps, filter_in, filter_mid, filter_out, decay_rate, skip_gain, out_weight, grad_out):

    def make_filter(first_w, middle_w, last_w):
        return filter_values(first_w, middle_w, last_w, decay_rate, SEQ)
    long_filter, pullback = jax.vjp(make_filter, filter_in, filter_mid, filter_out)
    filtered = short_apply(streams, short_taps)
    product = (filtered[1] * filtered[2]).astype(jnp.bfloat16)
    product_wide = product.astype(jnp.float32)
    long_out = causal_apply(long_filter, product_wide) + skip_gain[:, None] * product_wide
    gated_out = (filtered[0] * long_out).astype(jnp.bfloat16)
    layer_out = jnp.dot(out_weight, gated_out, preferred_element_type=jnp.float32).astype(jnp.bfloat16)
    grad_out_weight = jnp.dot(grad_out, gated_out.T, preferred_element_type=jnp.float32)
    grad_gated = jnp.dot(out_weight.T, grad_out, preferred_element_type=jnp.float32).astype(jnp.bfloat16)
    grad_gated_wide = grad_gated.astype(jnp.float32)
    grad_long = (grad_gated_wide * filtered[0]).astype(jnp.bfloat16)
    grad_long_wide = grad_long.astype(jnp.float32)
    grad_first = grad_gated_wide * long_out
    flipped = causal_apply(long_filter, jnp.flip(grad_long_wide, -1))
    grad_product = jnp.flip(flipped, -1) + skip_gain[:, None] * grad_long_wide
    grad_lag = correlate(grad_long_wide, product_wide)
    grad_filtered = jnp.stack([grad_first, grad_product * filtered[2], grad_product * filtered[1]])
    grad_streams = short_adjoint(grad_filtered, short_taps).astype(jnp.bfloat16)
    grad_filter_in, grad_filter_mid, grad_filter_out = pullback(grad_lag)
    return (layer_out, grad_streams, grad_filter_in, grad_filter_mid, grad_filter_out, grad_out_weight)
```

```python
import functools
import math

import jax
import jax.numpy as jnp
from jax import lax
from jax.experimental import pallas as pl
from jax.experimental.pallas import tpu as pltpu
from jax.sharding import PartitionSpec as P

precise = lax.Precision.HIGHEST
MESH = pl.DeviceIdType.MESH


def exchange_kernel(axis, peers, whole, *refs):
    count = len(whole)
    ins, outs = refs[:count], refs[count : 2 * count]
    send_sem, recv_sem, own_sem = refs[2 * count :]
    me = lax.axis_index(axis)
    barrier = pltpu.get_barrier_semaphore()
    for step in range(1, peers):
        pl.semaphore_signal(
            barrier, inc=1, device_id={axis: lax.rem(me + step, peers)}, device_id_type=MESH
        )
    pl.semaphore_wait(barrier, peers - 1)
    copies = []
    for k in range(count):
        for step in range(1, peers):
            peer = lax.rem(me + step, peers)
            copy = pltpu.make_async_remote_copy(
                src_ref=ins[k] if whole[k] else ins[k].at[peer],
                dst_ref=outs[k].at[me],
                send_sem=send_sem.at[k, step - 1],
                recv_sem=recv_sem.at[k, step - 1],
                device_id={axis: peer},
                device_id_type=MESH,
            )
            copy.start()
            copies.append(copy)
    for k in range(count):
        copy = pltpu.make_async_copy(
            ins[k] if whole[k] else ins[k].at[me], outs[k].at[me], own_sem.at[k]
        )
        copy.start()
        copies.append(copy)
    for copy in copies:
        copy.wait()


def exchange(axis, ident, arrays, whole):
    peers = lax.axis_size(axis)
    count = len(arrays)
    shapes = [
        jax.ShapeDtypeStruct(((peers,) + a.shape) if w else a.shape, a.dtype)
        for a, w in zip(arrays, whole)
    ]
    return pl.pallas_call(
        functools.partial(exchange_kernel, axis, peers, whole),
        out_shape=shapes,
        in_specs=[pl.BlockSpec(memory_space=pl.ANY)] * count,
        out_specs=[pl.BlockSpec(memory_space=pl.ANY)] * count,
        scratch_shapes=[
            pltpu.SemaphoreType.DMA((count, peers - 1)),
            pltpu.SemaphoreType.DMA((count, peers - 1)),
            pltpu.SemaphoreType.DMA((count,)),
        ],
        compiler_params=pltpu.CompilerParams(collective_id=ident, has_side_effects=True),
    )(*arrays)


def spread_kernel(lines, columns, parts, in_ref, out_ref, far_sem, mid_sem, near_sem, core_sem, recv_sem, own_sem):
    ch = lax.axis_index("ch")
    ctx = lax.axis_index("ctx")
    line, side = ch // 2, lax.rem(ch, 2)
    column, core = ctx // 2, lax.rem(ctx, 2)

    def at(line_to, side_to, column_to, core_to):
        return {"ch": line_to * 2 + side_to, "ctx": column_to * 2 + core_to}

    line_peers = [lax.rem(line + s, lines) for s in range(lines)]
    column_peers = [lax.rem(column + s, columns) for s in range(columns)]
    side_peers = [side, 1 - side]
    barrier = pltpu.get_barrier_semaphore()
    friends = [at(p, side, column, core) for p in line_peers[1:]]
    friends += [at(line, side, p, core) for p in column_peers[1:]]
    friends += [at(line, 1 - side, column, core), at(line, side, column, 1 - core)]
    for friend in friends:
        pl.semaphore_signal(barrier, inc=1, device_id=friend, device_id_type=MESH)
    pl.semaphore_wait(barrier, len(friends))

    pending = []

    def chunk(l, s, c, part):
        i, j = l * 2 + s, c * 2 + core
        first, rows = parts[part]
        return i, j, out_ref.at[i, j, pl.ds(first, rows)]

    def send(l, s, c, part, src, sem, target):
        i, j, dst = chunk(l, s, c, part)
        copy = pltpu.make_async_remote_copy(
            src_ref=dst if src is None else src,
            dst_ref=dst,
            send_sem=sem,
            recv_sem=recv_sem.at[i, j, part],
            device_id=target,
            device_id_type=MESH,
        )
        copy.start()
        pending.append(copy)

    def arrived(i, j, part):
        first, rows = parts[part]
        dst = out_ref.at[i, j, pl.ds(first, rows)]
        pltpu.make_async_copy(dst, dst, recv_sem.at[i, j, part]).wait()

    own = pltpu.make_async_copy(in_ref, out_ref.at[ch, ctx], own_sem)
    own.start()
    for part, (first, rows) in enumerate(parts):
        mine = in_ref.at[pl.ds(first, rows)]
        for s in range(1, lines):
            send(line, side, column, part, mine, far_sem.at[part, s], at(line_peers[s], side, column, core))
    sizes = [(2, columns), (columns, 2)]

    def coords(part, u, v):
        return (side_peers[u], column_peers[v]) if part == 0 else (side_peers[v], column_peers[u])

    def pass_on(part, l, u, v, src):
        s, c = coords(part, u, v)
        lp = line_peers[l]
        size_u, size_v = sizes[part]
        if u == 0 and v == 0:
            for w in range(1, size_u):
                ts, tc = coords(part, w, 0)
                send(lp, s, c, part, src, mid_sem.at[part, l, w], at(line, ts, tc, core))
        if v == 0:
            for w in range(1, size_v):
                ts, tc = coords(part, 0, w)
                send(lp, s, c, part, src, near_sem.at[part, l, u, w], at(line, ts, tc, core))
        send(lp, s, c, part, src, core_sem.at[part, l, u, v], at(line, side, column, 1 - core))

    def wait_for(part, l, u, v):
        s, c = coords(part, u, v)
        arrived(line_peers[l] * 2 + s, c * 2 + core, part)

    for l in range(lines):
        for part, (first, rows) in enumerate(parts):
            if l:
                wait_for(part, l, 0, 0)
            pass_on(part, l, 0, 0, None if l else in_ref.at[pl.ds(first, rows)])
        for part in range(len(parts)):
            for u in range(1, sizes[part][0]):
                wait_for(part, l, u, 0)
                pass_on(part, l, u, 0, None)
    for l in range(lines):
        for part in range(len(parts)):
            for u in range(sizes[part][0]):
                for v in range(1, sizes[part][1]):
                    wait_for(part, l, u, v)
                    pass_on(part, l, u, v, None)
    own.wait()
    for l in range(lines):
        for s in range(2):
            for c in range(columns):
                for part in range(len(parts)):
                    arrived(line_peers[l] * 2 + side_peers[s], column_peers[c] * 2 + (1 - core), part)
    for copy in pending:
        copy.wait_send()


def spread(ident, block):
    groups, cycle = lax.axis_size("ch"), lax.axis_size("ctx")
    rows, tokens = block.shape
    if groups * cycle > 64 or groups % 2 or cycle % 2:
        return lax.all_gather(lax.all_gather(block, "ctx"), "ch")
    cut = rows // 32 * 16
    parts = [(0, cut), (cut, rows - cut)] if cut else [(0, rows)]
    lines, columns = groups // 2, cycle // 2
    most = max(2, columns)
    count = len(parts)
    return pl.pallas_call(
        functools.partial(spread_kernel, lines, columns, parts),
        out_shape=jax.ShapeDtypeStruct((groups, cycle, rows, tokens), block.dtype),
        in_specs=[pl.BlockSpec(memory_space=pl.ANY)],
        out_specs=pl.BlockSpec(memory_space=pl.ANY),
        scratch_shapes=[
            pltpu.SemaphoreType.DMA((count, lines)),
            pltpu.SemaphoreType.DMA((count, lines, most)),
            pltpu.SemaphoreType.DMA((count, lines, most, most)),
            pltpu.SemaphoreType.DMA((count, lines, most, most)),
            pltpu.SemaphoreType.DMA((groups, cycle, count)),
            pltpu.SemaphoreType.DMA,
        ],
        compiler_params=pltpu.CompilerParams(collective_id=ident, has_side_effects=True),
    )(block)


def filter_values(filter_in, filter_mid, filter_out, decay_rate, length):
    band_count = filter_in.shape[0] // 2
    lag_index = jnp.arange(length)
    level_index = jnp.arange(1, band_count + 1)
    wrapped = level_index[:, None] * lag_index[None, :] % length
    phases = 2.0 * math.pi / length * wrapped.astype(jnp.float32)
    features = jnp.concatenate([jnp.cos(phases), jnp.sin(phases)], axis=0)
    hidden_one = jnp.sin(jnp.einsum("fh,fs->hs", filter_in, features, precision=precise))
    hidden_two = jnp.sin(jnp.einsum("gh,gs->hs", filter_mid, hidden_one, precision=precise))
    raw_out = jnp.einsum("hc,hs->cs", filter_out, hidden_two, precision=precise)
    lag_axis = lag_index.astype(jnp.float32)
    return (
        raw_out * jnp.exp(-decay_rate[:, None] * lag_axis[None, :]) * jnp.sqrt(decay_rate)[:, None]
    )


def fourier_tables(width_sub):
    double = 2 * width_sub
    row_index = jnp.arange(width_sub)
    col_index = jnp.arange(double)
    forward_phase = (
        2.0
        * math.pi
        / double
        * (row_index[:, None] * row_index[None, :] % double).astype(jnp.float32)
    )
    row_parity = (1 - 2 * (row_index % 2)).astype(jnp.float32)
    first_column = (row_index == 0)[None, :]
    forward_cos = jnp.cos(forward_phase)
    forward_sin = jnp.where(first_column, row_parity[:, None], -jnp.sin(forward_phase))
    inverse_phase = (
        2.0
        * math.pi
        / double
        * (row_index[:, None] * col_index[None, :] % double).astype(jnp.float32)
    )
    row_weight = jnp.where(row_index == 0, 1.0, 2.0).astype(jnp.float32)[:, None] / double
    col_parity = (1 - 2 * (col_index % 2)).astype(jnp.float32)
    inverse_cos = row_weight * jnp.cos(inverse_phase)
    inverse_sin = jnp.where(
        (row_index == 0)[:, None],
        col_parity[None, :] / double,
        -2.0 / double * jnp.sin(inverse_phase),
    )
    return (
        jnp.concatenate([forward_cos, forward_sin], axis=1),
        jnp.concatenate([inverse_cos, inverse_sin], axis=0),
    )


def spectral_product(left, right, width):
    lr, li = left[..., :width], left[..., width:]
    rr, ri = right[..., :width], right[..., width:]
    edge = lax.broadcasted_iota(jnp.int32, lr.shape, lr.ndim - 1) == 0
    cross = li * ri
    real = lr * rr - jnp.where(edge, 0.0, cross)
    imag = jnp.where(edge, cross, lr * ri + li * rr)
    return jnp.concatenate([real, imag], axis=-1)


def spectral_adjoint(left, right, width):
    lr, li = left[..., :width], left[..., width:]
    rr, ri = right[..., :width], right[..., width:]
    edge = lax.broadcasted_iota(jnp.int32, lr.shape, lr.ndim - 1) == 0
    cross = li * ri
    real = lr * rr + jnp.where(edge, 0.0, cross)
    imag = jnp.where(edge, cross, lr * ri - li * rr)
    return jnp.concatenate([real, imag], axis=-1)


def to_blocks(signal, blocks, width):
    return [signal[:, n * width : (n + 1) * width] for n in range(blocks)]


def transform(values, table):
    return jnp.dot(values, table, precision=precise)


def total(terms):
    terms = list(terms)
    value = terms[0]
    for term in terms[1:]:
        value = value + term
    return value


def short_apply(signal, taps):
    wide = signal.astype(jnp.float32)
    out = taps[..., 0:1] * wide
    for lag in range(1, taps.shape[-1]):
        moved = jnp.pad(wide, ((0, 0), (0, 0), (lag, 0)))[:, :, : wide.shape[2]]
        out = out + taps[..., lag : lag + 1] * moved
    return out


def short_adjoint(signal, taps):
    out = taps[..., 0:1] * signal
    for lag in range(1, taps.shape[-1]):
        moved = jnp.pad(signal, ((0, 0), (0, 0), (0, lag)))[:, :, lag:]
        out = out + taps[..., lag : lag + 1] * moved
    return out


def shards(
    streams,
    short_taps,
    filter_in,
    filter_mid,
    filter_out,
    decay_rate,
    skip_gain,
    out_weight,
    grad_out,
):
    channels, tokens = streams.shape[1:]
    cycle, groups = lax.axis_size("ctx"), lax.axis_size("ch")
    ctx = lax.axis_index("ctx")
    length = tokens * cycle
    share = channels // cycle
    width = min(256, tokens)
    blocks = length // width
    forward, inverse = fourier_tables(width)

    def mine(value, axis):
        return lax.dynamic_slice_in_dim(value, ctx * share, share, axis)

    pieces = streams.reshape(3, cycle, share, tokens).transpose(1, 0, 2, 3)
    pieces, grad_all = exchange("ctx", 0, [pieces, grad_out], [False, True])
    grad_all = grad_all.transpose(1, 0, 2).reshape(grad_out.shape[0], length)
    whole = pieces.transpose(1, 2, 0, 3).reshape(3, share, length)

    columns = lax.dynamic_index_in_dim(
        out_weight.reshape(out_weight.shape[0], groups, cycle, share), ctx, 2, False
    )
    terms = jnp.einsum("dgc,dt->gct", columns, grad_all, preferred_element_type=jnp.float32)
    (terms,) = exchange("ch", 1, [terms.astype(jnp.bfloat16)], [False])

    taps = mine(short_taps, 1)
    skip = mine(skip_gain, 0)[:, None]
    rate = mine(decay_rate, 0)

    def make_filter(first_w, middle_w, last_w):
        return filter_values(first_w, middle_w, last_w, rate, length)

    long_filter, pullback = jax.vjp(make_filter, filter_in, filter_mid, mine(filter_out, 1))
    filtered = short_apply(whole, taps)
    product = (filtered[1] * filtered[2]).astype(jnp.bfloat16).astype(jnp.float32)

    lag_spec = [transform(b, forward) for b in to_blocks(long_filter, blocks, width)]
    own_spec = [transform(b, forward) for b in to_blocks(product, blocks, width)]
    out_blocks = []
    carry = 0.0
    for k in range(blocks):
        spec = total(spectral_product(lag_spec[i], own_spec[k - i], width) for i in range(k + 1))
        double = transform(spec, inverse)
        out_blocks.append(double[:, :width] + carry)
        carry = double[:, width:]
    long_out = jnp.concatenate(out_blocks, axis=1) + skip * product
    gated_out = (filtered[0] * long_out).astype(jnp.bfloat16)

    gated = spread(2, gated_out).reshape(groups * channels, length)
    here = lax.dynamic_slice_in_dim(gated, ctx * tokens, tokens, 1)
    layer_out = jnp.dot(out_weight, here, preferred_element_type=jnp.float32).astype(jnp.bfloat16)
    weight_grad = jnp.einsum("dt,ct->dc", grad_all, gated, preferred_element_type=jnp.float32)

    grad_gated = jnp.sum(terms.astype(jnp.float32), axis=0).astype(jnp.bfloat16).astype(jnp.float32)
    grad_long = (grad_gated * filtered[0]).astype(jnp.bfloat16).astype(jnp.float32)
    grad_first = grad_gated * long_out
    grad_blocks = to_blocks(grad_long, blocks, width)
    grad_spec = []
    for k in range(blocks):
        after = grad_blocks[k + 1] if k + 1 < blocks else jnp.zeros_like(grad_blocks[k])
        grad_spec.append(transform(jnp.concatenate([grad_blocks[k], after], axis=1), inverse.T))
    back_blocks, lag_blocks = [], []
    for j in range(blocks):
        back = total(spectral_adjoint(lag_spec[k - j], grad_spec[k], width) for k in range(j, blocks))
        lags = total(spectral_adjoint(own_spec[k - j], grad_spec[k], width) for k in range(j, blocks))
        back_blocks.append(transform(back, forward.T))
        lag_blocks.append(transform(lags, forward.T))
    grad_product = jnp.concatenate(back_blocks, axis=1) + skip * grad_long
    grad_lag = jnp.concatenate(lag_blocks, axis=1)
    grad_filtered = jnp.stack([grad_first, grad_product * filtered[2], grad_product * filtered[1]])
    grad_streams = short_adjoint(grad_filtered, taps).astype(jnp.bfloat16)
    grad_in, grad_mid, grad_last = pullback(grad_lag)

    pieces = grad_streams.reshape(3, share, cycle, tokens).transpose(2, 0, 1, 3)
    small = jnp.concatenate([grad_in, grad_mid], axis=0)
    pieces, grad_last, small = exchange(
        "ctx", 3, [pieces, grad_last.T, small], [False, True, True]
    )
    grad_streams = pieces.transpose(1, 0, 2, 3).reshape(streams.shape)
    grad_filter_out = grad_last.reshape(channels, filter_out.shape[0]).T
    (small,) = exchange("ch", 4, [jnp.sum(small, axis=0)], [True])
    small = jnp.sum(small, axis=0)
    cut = filter_in.shape[0]
    return (layer_out, grad_streams, small[:cut], small[cut:], grad_filter_out, weight_grad)


def solution(mesh):
    return jax.shard_map(
        shards,
        mesh=mesh,
        in_specs=(
            P(None, "ch", "ctx"),
            P(None, "ch", None),
            P(),
            P(),
            P(None, "ch"),
            P("ch"),
            P("ch"),
            P("ch", None),
            P("ch", "ctx"),
        ),
        out_specs=(P("ch", "ctx"), P(None, "ch", "ctx"), P(), P(), P(None, "ch"), P("ch", None)),
        check_vma=False,
    )
```

```python
import functools
import math

import jax
import jax.numpy as jnp
import numpy as np
from jax import lax
from jax.experimental import pallas as pl
from jax.experimental.pallas import tpu as pltpu
from jax.sharding import PartitionSpec as P

precise = lax.Precision.HIGHEST
MESH = pl.DeviceIdType.MESH


def arrived(ref, sem):
    pltpu.make_async_copy(ref, ref, sem).wait()


def greet(friends):
    barrier = pltpu.get_barrier_semaphore()
    for friend in friends:
        pl.semaphore_signal(barrier, inc=1, device_id=friend, device_id_type=MESH)
    pl.semaphore_wait(barrier, len(friends))


def remote(src, dst, send_sem, recv_sem, target):
    copy = pltpu.make_async_remote_copy(
        src_ref=src,
        dst_ref=dst,
        send_sem=send_sem,
        recv_sem=recv_sem,
        device_id=target,
        device_id_type=MESH,
    )
    copy.start()
    return copy


def in_any(count):
    return [pl.BlockSpec(memory_space=pl.ANY)] * count


def to_sequence_kernel(cycle, tokens, in_ref, out_ref, send_sem, recv_sem, own_sem):
    me = lax.axis_index("ctx")
    peers = [lax.rem(me + step, cycle) for step in range(cycle)]
    greet([{"ctx": peer} for peer in peers[1:]])
    place = out_ref.at[:, :, pl.ds(pl.multiple_of(me * tokens, tokens), tokens)]
    copies = [
        remote(in_ref.at[:, peers[s]], place, send_sem.at[s], recv_sem.at[s], {"ctx": peers[s]})
        for s in range(1, cycle)
    ]
    own = pltpu.make_async_copy(in_ref.at[:, me], place, own_sem)
    own.start()
    own.wait()
    for copy in copies:
        copy.wait()


def to_sequence(ident, pieces):
    streams, cycle, share, tokens = pieces.shape
    return pl.pallas_call(
        functools.partial(to_sequence_kernel, cycle, tokens),
        out_shape=jax.ShapeDtypeStruct((streams, share, cycle * tokens), pieces.dtype),
        in_specs=in_any(1),
        out_specs=pl.BlockSpec(memory_space=pl.ANY),
        scratch_shapes=[
            pltpu.SemaphoreType.DMA((cycle,)),
            pltpu.SemaphoreType.DMA((cycle,)),
            pltpu.SemaphoreType.DMA,
        ],
        compiler_params=pltpu.CompilerParams(collective_id=ident, has_side_effects=True),
    )(pieces)


def finish_kernel(
    cycle, groups, tokens, seq_ref, last_ref, small_ref, out_ref, last_out, small_out,
    from_ctx, mine, from_ch, send_sem, recv_sem, own_sem, ch_send, ch_recv,
):
    me, group = lax.axis_index("ctx"), lax.axis_index("ch")
    peers = [lax.rem(me + step, cycle) for step in range(cycle)]
    others = [lax.rem(group + step, groups) for step in range(groups)]
    greet([{"ctx": p} for p in peers[1:]] + [{"ch": p} for p in others[1:]])
    small_copies, copies = [], []
    for s in range(1, cycle):
        to = {"ctx": peers[s]}
        small_copies.append(
            remote(small_ref, from_ctx.at[me], send_sem.at[0, s], recv_sem.at[0, s], to)
        )
    for s in range(1, cycle):
        to = {"ctx": peers[s]}
        src = seq_ref.at[:, :, pl.ds(pl.multiple_of(peers[s] * tokens, tokens), tokens)]
        copies.append(remote(src, out_ref.at[:, me], send_sem.at[1, s], recv_sem.at[1, s], to))
        copies.append(remote(last_ref, last_out.at[me], send_sem.at[2, s], recv_sem.at[2, s], to))
    src = seq_ref.at[:, :, pl.ds(pl.multiple_of(me * tokens, tokens), tokens)]
    owns = [
        pltpu.make_async_copy(src, out_ref.at[:, me], own_sem.at[0]),
        pltpu.make_async_copy(last_ref, last_out.at[me], own_sem.at[1]),
    ]
    for own in owns:
        own.start()
    from_ctx[me] = small_ref[...]
    for copy in small_copies:
        copy.wait()
    mine[...] = total(from_ctx[j] for j in range(cycle))
    small_copies = [
        remote(mine, from_ch.at[group], ch_send.at[s], ch_recv.at[s], {"ch": others[s]})
        for s in range(1, groups)
    ]
    from_ch[group] = mine[...]
    for copy in small_copies:
        copy.wait()
    small_out[...] = total(from_ch[i] for i in range(groups))
    for copy in owns + copies:
        copy.wait()


def finish(ident, seq, last, small, tokens):
    cycle, groups = lax.axis_size("ctx"), lax.axis_size("ch")
    streams, share, _ = seq.shape
    vmem = pl.BlockSpec(memory_space=pltpu.VMEM)
    return pl.pallas_call(
        functools.partial(finish_kernel, cycle, groups, tokens),
        out_shape=[
            jax.ShapeDtypeStruct((streams, cycle, share, tokens), seq.dtype),
            jax.ShapeDtypeStruct((cycle,) + last.shape, last.dtype),
            jax.ShapeDtypeStruct(small.shape, small.dtype),
        ],
        in_specs=in_any(2) + [vmem],
        out_specs=in_any(2) + [vmem],
        scratch_shapes=[
            pltpu.VMEM((cycle,) + small.shape, small.dtype),
            pltpu.VMEM(small.shape, small.dtype),
            pltpu.VMEM((groups,) + small.shape, small.dtype),
            pltpu.SemaphoreType.DMA((3, cycle)),
            pltpu.SemaphoreType.DMA((3, cycle)),
            pltpu.SemaphoreType.DMA((2,)),
            pltpu.SemaphoreType.DMA((groups,)),
            pltpu.SemaphoreType.DMA((groups,)),
        ],
        compiler_params=pltpu.CompilerParams(collective_id=ident, has_side_effects=True),
    )(seq, last, small)


def middle_kernel(
    lines, columns, parts, tokens, share,
    terms_ref, cot_ref, in_ref, sum_ref, cot_out, out_ref,
    side_buf, half_buf, line_buf, ready,
    side_send, side_recv, line_send, line_recv, ready_send, ready_recv,
    cot_send, cot_recv, far_sem, mid_sem, near_sem, core_sem, recv_sem, own_sem,
):
    ch = lax.axis_index("ch")
    ctx = lax.axis_index("ctx")
    cycle = columns * 2
    line, side = ch // 2, lax.rem(ch, 2)
    column, core = ctx // 2, lax.rem(ctx, 2)

    def at(line_to, side_to, column_to, core_to):
        return {"ch": line_to * 2 + side_to, "ctx": column_to * 2 + core_to}

    line_peers = [lax.rem(line + s, lines) for s in range(lines)]
    column_peers = [lax.rem(column + s, columns) for s in range(columns)]
    ctx_peers = [lax.rem(ctx + s, cycle) for s in range(cycle)]
    side_peers = [side, 1 - side]
    greet(
        [at(p, side, column, core) for p in line_peers[1:]]
        + [at(line, 1 - side, column, core)]
        + [{"ctx": p} for p in ctx_peers[1:]]
    )
    pending = []

    for s in [*range(1, lines), 0]:
        l = line_peers[s]
        pending.append(
            remote(
                terms_ref.at[l * 2 + 1 - side], side_buf.at[l], side_send.at[s], side_recv.at[l],
                at(line, 1 - side, column, core),
            )
        )

    def halves(s):
        l = line_peers[s]
        arrived(side_buf.at[l], side_recv.at[l])
        return terms_ref[l * 2 + side].astype(jnp.float32) + side_buf[l].astype(jnp.float32)

    def send_half(s):
        half_buf[s] = halves(s).astype(half_buf.dtype)
        pending.append(
            remote(
                half_buf.at[s], line_buf.at[line], line_send.at[s], line_recv.at[line],
                at(line_peers[s], side, column, core),
            )
        )

    def finish_sum():
        value = halves(0)
        for s in range(1, lines):
            l = line_peers[s]
            arrived(line_buf.at[l], line_recv.at[l])
            value = value + line_buf[l].astype(jnp.float32)
        value = value.astype(ready.dtype)
        for j in range(cycle):
            ready[j] = value[j * share : (j + 1) * share]
        place = sum_ref.at[:, pl.ds(pl.multiple_of(ctx * tokens, tokens), tokens)]
        copies = [
            remote(
                ready.at[ctx_peers[s]], place, ready_send.at[s], ready_recv.at[s],
                {"ctx": ctx_peers[s]},
            )
            for s in range(1, cycle)
        ]
        own = pltpu.make_async_copy(ready.at[ctx], place, own_sem.at[1])
        own.start()
        return copies + [own]

    def cot_place(j):
        return cot_out.at[:, pl.ds(pl.multiple_of(j * tokens, tokens), tokens)]

    for s in range(1, columns):
        pending.append(
            remote(
                cot_ref, cot_place(ctx), cot_send.at[0, s], cot_recv.at[ctx],
                at(line, side, column_peers[s], core),
            )
        )
    owns = [pltpu.make_async_copy(cot_ref, cot_place(ctx), own_sem.at[2])]
    owns[0].start()

    def pass_cot(s):
        j = column_peers[s] * 2 + core
        if s:
            arrived(cot_place(j), cot_recv.at[j])
        pending.append(
            remote(
                cot_place(j) if s else cot_ref, cot_place(j), cot_send.at[1, s], cot_recv.at[j],
                at(line, side, column, 1 - core),
            )
        )

    def chunk(i, j, part):
        first, rows = parts[part]
        return out_ref.at[i, j, pl.ds(first, rows)]

    def send(l, s, c, part, src, sem, target):
        i, j = l * 2 + s, c * 2 + core
        dst = chunk(i, j, part)
        pending.append(remote(dst if src is None else src, dst, sem, recv_sem.at[i, j, part], target))

    sizes = [(2, columns), (columns, 2)]

    def coords(part, u, v):
        return (side_peers[u], column_peers[v]) if part == 0 else (side_peers[v], column_peers[u])

    def pass_on(part, l, u, v, src):
        s, c = coords(part, u, v)
        lp = line_peers[l]
        size_u, size_v = sizes[part]
        if u == 0 and v == 0:
            for w in range(1, size_u):
                ts, tc = coords(part, w, 0)
                send(lp, s, c, part, src, mid_sem.at[part, l, w], at(line, ts, tc, core))
        if v == 0:
            for w in range(1, size_v):
                ts, tc = coords(part, 0, w)
                send(lp, s, c, part, src, near_sem.at[part, l, u, w], at(line, ts, tc, core))
        send(lp, s, c, part, src, core_sem.at[part, l, u, v], at(line, side, column, 1 - core))

    def wait_for(part, l, u, v):
        s, c = coords(part, u, v)
        i, j = line_peers[l] * 2 + s, c * 2 + core
        arrived(chunk(i, j, part), recv_sem.at[i, j, part])

    if parts:
        own = pltpu.make_async_copy(in_ref, out_ref.at[ch, ctx], own_sem.at[0])
        own.start()
        owns.append(own)
    for part, (first, rows) in enumerate(parts):
        mine = in_ref.at[pl.ds(first, rows)]
        for s in range(1, lines):
            send(
                line, side, column, part, mine, far_sem.at[part, s],
                at(line_peers[s], side, column, core),
            )
    pass_cot(0)
    for l in range(lines):
        for part, (first, rows) in enumerate(parts):
            if l:
                wait_for(part, l, 0, 0)
            pass_on(part, l, 0, 0, None if l else in_ref.at[pl.ds(first, rows)])
        if l + 1 < lines:
            send_half(l + 1)
    for s in range(1, columns):
        pass_cot(s)
    for l in range(lines):
        for part in range(len(parts)):
            for u in range(1, sizes[part][0]):
                wait_for(part, l, u, 0)
                pass_on(part, l, u, 0, None)
    sums = finish_sum()
    for l in range(lines):
        for part in range(len(parts)):
            for u in range(sizes[part][0]):
                for v in range(1, sizes[part][1]):
                    wait_for(part, l, u, v)
                    pass_on(part, l, u, v, None)
    for copy in owns + sums:
        copy.wait()
    for s in range(columns):
        j = column_peers[s] * 2 + 1 - core
        arrived(cot_place(j), cot_recv.at[j])
    for part in range(len(parts)):
        for l in range(lines):
            for s in range(2):
                for c in range(columns):
                    i, j = line_peers[l] * 2 + side_peers[s], column_peers[c] * 2 + (1 - core)
                    arrived(chunk(i, j, part), recv_sem.at[i, j, part])
    for copy in pending:
        copy.wait_send()


def middle(ident, terms, cot, block):
    groups, cycle = lax.axis_size("ch"), lax.axis_size("ctx")
    _, channels, tokens = terms.shape
    share, length = block.shape
    lines, columns = groups // 2, cycle // 2
    cut = share // 16 * 13 // 16 * 16
    parts = [(0, cut), (cut, share - cut)] if 0 < cut < share else [(0, share)]
    if groups * cycle > 64:
        parts = []
    most = max(2, columns)
    count = max(1, len(parts))
    spread_shape = (groups, cycle, share, length) if parts else (1, 1, 8, 128)
    dma = pltpu.SemaphoreType.DMA
    summed, cot_all, spread = pl.pallas_call(
        functools.partial(middle_kernel, lines, columns, parts, tokens, share),
        out_shape=[
            jax.ShapeDtypeStruct((share, length), terms.dtype),
            jax.ShapeDtypeStruct((cot.shape[0], length), cot.dtype),
            jax.ShapeDtypeStruct(spread_shape, block.dtype),
        ],
        in_specs=[pl.BlockSpec(memory_space=pltpu.VMEM)] + in_any(2),
        out_specs=in_any(3),
        scratch_shapes=[
            pltpu.VMEM((lines, channels, tokens), terms.dtype),
            pltpu.VMEM((lines, channels, tokens), terms.dtype),
            pltpu.VMEM((lines, channels, tokens), terms.dtype),
            pltpu.VMEM((cycle, share, tokens), terms.dtype),
            dma((lines,)),
            dma((lines,)),
            dma((lines,)),
            dma((lines,)),
            dma((cycle,)),
            dma((cycle,)),
            dma((2, columns)),
            dma((cycle,)),
            dma((count, lines)),
            dma((count, lines, most)),
            dma((count, lines, most, most)),
            dma((count, lines, most, most)),
            dma((groups if parts else 1, cycle, count)),
            dma((3,)),
        ],
        compiler_params=pltpu.CompilerParams(
            collective_id=ident, has_side_effects=True, vmem_limit_bytes=48 * 2**20
        ),
    )(terms, cot, block)
    if not parts:
        spread = lax.all_gather(lax.all_gather(block, "ctx"), "ch")
    return summed, cot_all, spread


def filter_values(filter_in, filter_mid, filter_out, decay_rate, length):
    band_count = filter_in.shape[0] // 2
    lag_index = np.arange(length)
    phases = 2.0 * math.pi / length * (np.arange(1, band_count + 1)[:, None] * lag_index % length)
    features = jnp.asarray(np.concatenate([np.cos(phases), np.sin(phases)]), jnp.float32)
    hidden_one = jnp.sin(jnp.einsum("fh,fs->hs", filter_in, features, precision=precise))
    hidden_two = jnp.sin(jnp.einsum("gh,gs->hs", filter_mid, hidden_one, precision=precise))
    raw_out = jnp.einsum("hc,hs->cs", filter_out, hidden_two, precision=precise)
    lag_axis = jnp.arange(length).astype(jnp.float32)
    return (
        raw_out * jnp.exp(-decay_rate[:, None] * lag_axis[None, :]) * jnp.sqrt(decay_rate)[:, None]
    )


def fourier_tables(width):
    double = 2 * width
    row, col = np.arange(width), np.arange(double)
    phase = 2.0 * math.pi / double * (row[:, None] * row[None, :] % double)
    forward_cos = np.cos(phase)
    forward_sin = np.where(row[None, :] == 0, (1 - 2 * (row % 2))[:, None], -np.sin(phase))
    phase = 2.0 * math.pi / double * (row[:, None] * col[None, :] % double)
    inverse_cos = np.where(row == 0, 1.0, 2.0)[:, None] / double * np.cos(phase)
    inverse_sin = np.where(
        row[:, None] == 0, (1 - 2 * (col % 2))[None, :] / double, -2.0 / double * np.sin(phase)
    )
    return (
        np.concatenate([forward_cos, forward_sin], axis=1).astype(np.float32),
        np.concatenate([inverse_cos, inverse_sin], axis=0).astype(np.float32),
    )


def spectral_product(left, right, width):
    lr, li = left[..., :width], left[..., width:]
    rr, ri = right[..., :width], right[..., width:]
    edge = lax.broadcasted_iota(jnp.int32, lr.shape, lr.ndim - 1) == 0
    cross = li * ri
    real = lr * rr - jnp.where(edge, 0.0, cross)
    imag = jnp.where(edge, cross, lr * ri + li * rr)
    return jnp.concatenate([real, imag], axis=-1)


def spectral_adjoint(left, right, width):
    lr, li = left[..., :width], left[..., width:]
    rr, ri = right[..., :width], right[..., width:]
    edge = lax.broadcasted_iota(jnp.int32, lr.shape, lr.ndim - 1) == 0
    cross = li * ri
    real = lr * rr + jnp.where(edge, 0.0, cross)
    imag = jnp.where(edge, cross, lr * ri - li * rr)
    return jnp.concatenate([real, imag], axis=-1)


def to_blocks(signal, blocks, width):
    return [signal[:, n * width : (n + 1) * width] for n in range(blocks)]


def transform(values, table):
    return jnp.dot(values, table, precision=precise)


def total(terms):
    terms = list(terms)
    value = terms[0]
    for term in terms[1:]:
        value = value + term
    return value


def short_apply(signal, taps):
    wide = signal.astype(jnp.float32)
    out = taps[..., 0:1] * wide
    for lag in range(1, taps.shape[-1]):
        moved = jnp.pad(wide, ((0, 0), (0, 0), (lag, 0)))[:, :, : wide.shape[2]]
        out = out + taps[..., lag : lag + 1] * moved
    return out


def short_adjoint(signal, taps):
    out = taps[..., 0:1] * signal
    for lag in range(1, taps.shape[-1]):
        moved = jnp.pad(signal, ((0, 0), (0, 0), (0, lag)))[:, :, lag:]
        out = out + taps[..., lag : lag + 1] * moved
    return out


def shards(
    streams,
    short_taps,
    filter_in,
    filter_mid,
    filter_out,
    decay_rate,
    skip_gain,
    out_weight,
    grad_out,
):
    channels, tokens = streams.shape[1:]
    cycle, groups = lax.axis_size("ctx"), lax.axis_size("ch")
    ctx = lax.axis_index("ctx")
    length = tokens * cycle
    share = channels // cycle
    width = min(256, tokens)
    blocks = length // width
    forward, inverse = fourier_tables(width)

    def mine(value, axis):
        return lax.dynamic_slice_in_dim(value, ctx * share, share, axis)

    whole = to_sequence(0, streams.reshape(3, cycle, share, tokens))
    terms = jnp.einsum("dc,dt->ct", out_weight, grad_out, preferred_element_type=jnp.float32)
    terms = terms.astype(jnp.bfloat16).reshape(groups, channels, tokens)

    taps = mine(short_taps, 1)
    skip = mine(skip_gain, 0)[:, None]
    rate = mine(decay_rate, 0)

    def make_filter(first_w, middle_w, last_w):
        return filter_values(first_w, middle_w, last_w, rate, length)

    long_filter, pullback = jax.vjp(make_filter, filter_in, filter_mid, mine(filter_out, 1))
    filtered = short_apply(whole, taps)
    product = (filtered[1] * filtered[2]).astype(jnp.bfloat16).astype(jnp.float32)

    lag_spec = [transform(b, forward) for b in to_blocks(long_filter, blocks, width)]
    own_spec = [transform(b, forward) for b in to_blocks(product, blocks, width)]
    out_blocks = []
    carry = 0.0
    for k in range(blocks):
        spec = total(spectral_product(lag_spec[i], own_spec[k - i], width) for i in range(k + 1))
        double = transform(spec, inverse)
        out_blocks.append(double[:, :width] + carry)
        carry = double[:, width:]
    long_out = jnp.concatenate(out_blocks, axis=1) + skip * product
    gated_out = (filtered[0] * long_out).astype(jnp.bfloat16)

    grad_gated, grad_all, gated = middle(1, terms, grad_out, gated_out)
    gated = gated.reshape(groups * channels, length)
    here = lax.dynamic_slice_in_dim(gated, ctx * tokens, tokens, 1)
    layer_out = jnp.dot(out_weight, here, preferred_element_type=jnp.float32).astype(jnp.bfloat16)
    weight_grad = jnp.einsum("dt,ct->dc", grad_all, gated, preferred_element_type=jnp.float32)

    grad_gated = grad_gated.astype(jnp.float32)
    grad_long = (grad_gated * filtered[0]).astype(jnp.bfloat16).astype(jnp.float32)
    grad_first = grad_gated * long_out
    grad_blocks = to_blocks(grad_long, blocks, width)
    grad_spec = []
    for k in range(blocks):
        after = grad_blocks[k + 1] if k + 1 < blocks else jnp.zeros_like(grad_blocks[k])
        grad_spec.append(transform(jnp.concatenate([grad_blocks[k], after], axis=1), inverse.T))
    back_blocks, lag_blocks = [], []
    for j in range(blocks):
        back = total(spectral_adjoint(lag_spec[k - j], grad_spec[k], width) for k in range(j, blocks))
        lags = total(spectral_adjoint(own_spec[k - j], grad_spec[k], width) for k in range(j, blocks))
        back_blocks.append(transform(back, forward.T))
        lag_blocks.append(transform(lags, forward.T))
    grad_product = jnp.concatenate(back_blocks, axis=1) + skip * grad_long
    grad_lag = jnp.concatenate(lag_blocks, axis=1)
    grad_filtered = jnp.stack([grad_first, grad_product * filtered[2], grad_product * filtered[1]])
    grad_streams = short_adjoint(grad_filtered, taps).astype(jnp.bfloat16)
    grad_in, grad_mid, grad_last = pullback(grad_lag)

    small = jnp.concatenate([grad_in, grad_mid], axis=0).reshape(-1, 128)
    grad_streams, grad_last, small = finish(2, grad_streams, grad_last.T, small, tokens)
    grad_streams = grad_streams.reshape(streams.shape)
    grad_filter_out = grad_last.reshape(channels, filter_out.shape[0]).T
    small = small.reshape(-1, filter_in.shape[1])
    cut = filter_in.shape[0]
    return (layer_out, grad_streams, small[:cut], small[cut:], grad_filter_out, weight_grad)


def solution(mesh):
    return jax.shard_map(
        shards,
        mesh=mesh,
        in_specs=(
            P(None, "ch", "ctx"),
            P(None, "ch", None),
            P(),
            P(),
            P(None, "ch"),
            P("ch"),
            P("ch"),
            P("ch", None),
            P("ch", "ctx"),
        ),
        out_specs=(P("ch", "ctx"), P(None, "ch", "ctx"), P(), P(), P(None, "ch"), P("ch", None)),
        check_vma=False,
    )
```

```python
import functools
import math

import jax
import jax.numpy as jnp
import numpy as np
from jax import lax
from jax.experimental import pallas as pl
from jax.experimental.pallas import tpu as pltpu
from jax.sharding import PartitionSpec as P

precise = lax.Precision.HIGHEST
MESH = pl.DeviceIdType.MESH


def arrived(ref, sem):
    pltpu.make_async_copy(ref, ref, sem).wait()


def greet(friends):
    barrier = pltpu.get_barrier_semaphore()
    for friend in friends:
        pl.semaphore_signal(barrier, inc=1, device_id=friend, device_id_type=MESH)
    pl.semaphore_wait(barrier, len(friends))


def remote(src, dst, send_sem, recv_sem, target):
    copy = pltpu.make_async_remote_copy(
        src_ref=src,
        dst_ref=dst,
        send_sem=send_sem,
        recv_sem=recv_sem,
        device_id=target,
        device_id_type=MESH,
    )
    copy.start()
    return copy


def in_any(count):
    return [pl.BlockSpec(memory_space=pl.ANY)] * count


def layer_kernel(
    lines, columns, parts, tokens, share, width,
    streams_ref, terms_ref, cot_ref, taps_ref, skip_ref, env_ref, last_ref, last_flat_ref,
    mid_ref, one_ref, one_slope_ref, two_ref, two_slope_ref, features_ref, forward_ref, inverse_ref,
    gated_ref, cot_out, out_ref, back_out, last_out, small_out,
    seq, filtered, product, long_out, lag_spec, own_spec, sum_ref, back_seq, last_own,
    small_own, from_ctx, small_sum, from_ch,
    side_buf, half_buf, line_buf, ready,
    seq_send, seq_recv, side_send, side_recv, line_send, line_recv, ready_send, ready_recv,
    cot_send, cot_recv, far_sem, mid_sem, near_sem, core_sem, recv_sem, own_sem,
    back_send, back_recv, ch_send, ch_recv,
):
    ch = lax.axis_index("ch")
    ctx = lax.axis_index("ctx")
    cycle = columns * 2
    line, side = ch // 2, lax.rem(ch, 2)
    column, core = ctx // 2, lax.rem(ctx, 2)

    def at(line_to, side_to, column_to, core_to):
        return {"ch": line_to * 2 + side_to, "ctx": column_to * 2 + core_to}

    line_peers = [lax.rem(line + s, lines) for s in range(lines)]
    column_peers = [lax.rem(column + s, columns) for s in range(columns)]
    ctx_peers = [lax.rem(ctx + s, cycle) for s in range(cycle)]
    side_peers = [side, 1 - side]
    groups = lines * 2
    ch_peers = [lax.rem(ch + s, groups) for s in range(groups)]
    greet([{"ctx": p} for p in ctx_peers[1:]] + [{"ch": p} for p in ch_peers[1:]])
    pending = []
    blocks = cycle * tokens // width

    def span(j):
        return pl.ds(pl.multiple_of(j * tokens, tokens), tokens)

    seq_copies = [
        remote(
            streams_ref.at[:, ctx_peers[s]], seq.at[:, :, span(ctx)], seq_send.at[s], seq_recv.at[s],
            {"ctx": ctx_peers[s]},
        )
        for s in range(1, cycle)
    ]
    seq_copies.append(
        pltpu.make_async_copy(streams_ref.at[:, ctx], seq.at[:, :, span(ctx)], own_sem.at[3])
    )
    seq_copies[-1].start()

    for s in [*range(1, lines), 0]:
        l = line_peers[s]
        pending.append(
            remote(
                terms_ref.at[l * 2 + 1 - side], side_buf.at[l], side_send.at[s], side_recv.at[l],
                at(line, 1 - side, column, core),
            )
        )

    def halves(s):
        l = line_peers[s]
        arrived(side_buf.at[l], side_recv.at[l])
        return terms_ref[l * 2 + side].astype(jnp.float32) + side_buf[l].astype(jnp.float32)

    def send_half(s):
        half_buf[s] = halves(s).astype(half_buf.dtype)
        pending.append(
            remote(
                half_buf.at[s], line_buf.at[line], line_send.at[s], line_recv.at[line],
                at(line_peers[s], side, column, core),
            )
        )

    def finish_sum():
        value = halves(0)
        for s in range(1, lines):
            l = line_peers[s]
            arrived(line_buf.at[l], line_recv.at[l])
            value = value + line_buf[l].astype(jnp.float32)
        value = value.astype(ready.dtype)
        if ready.shape[1] != share:
            ready[...] = jnp.zeros(ready.shape, ready.dtype)
        for j in range(cycle):
            ready[j, :share] = value[j * share : (j + 1) * share]
        place = sum_ref.at[:, pl.ds(pl.multiple_of(ctx * tokens, tokens), tokens)]
        copies = [
            remote(
                ready.at[ctx_peers[s]], place, ready_send.at[s], ready_recv.at[s],
                {"ctx": ctx_peers[s]},
            )
            for s in range(1, cycle)
        ]
        own = pltpu.make_async_copy(ready.at[ctx], place, own_sem.at[1])
        own.start()
        return copies + [own]

    def cot_place(j):
        return cot_out.at[:, pl.ds(pl.multiple_of(j * tokens, tokens), tokens)]

    for s in range(1, columns):
        pending.append(
            remote(
                cot_ref, cot_place(ctx), cot_send.at[0, s], cot_recv.at[ctx],
                at(line, side, column_peers[s], core),
            )
        )
    owns = [pltpu.make_async_copy(cot_ref, cot_place(ctx), own_sem.at[2])]
    owns[0].start()

    def pass_cot(s):
        j = column_peers[s] * 2 + core
        if s:
            arrived(cot_place(j), cot_recv.at[j])
        pending.append(
            remote(
                cot_place(j) if s else cot_ref, cot_place(j), cot_send.at[1, s], cot_recv.at[j],
                at(line, side, column, 1 - core),
            )
        )

    def chunk(i, j, part):
        first, rows = parts[part]
        return out_ref.at[i, j, pl.ds(first, rows)]

    def send(l, s, c, part, src, sem, target):
        i, j = l * 2 + s, c * 2 + core
        dst = chunk(i, j, part)
        pending.append(remote(dst if src is None else src, dst, sem, recv_sem.at[i, j, part], target))

    sizes = [(2, columns), (columns, 2)]

    def coords(part, u, v):
        return (side_peers[u], column_peers[v]) if part == 0 else (side_peers[v], column_peers[u])

    def pass_on(part, l, u, v, src):
        s, c = coords(part, u, v)
        lp = line_peers[l]
        size_u, size_v = sizes[part]
        if u == 0 and v == 0:
            for w in range(1, size_u):
                ts, tc = coords(part, w, 0)
                send(lp, s, c, part, src, mid_sem.at[part, l, w], at(line, ts, tc, core))
        if v == 0:
            for w in range(1, size_v):
                ts, tc = coords(part, 0, w)
                send(lp, s, c, part, src, near_sem.at[part, l, u, w], at(line, ts, tc, core))
        send(lp, s, c, part, src, core_sem.at[part, l, u, v], at(line, side, column, 1 - core))

    def wait_for(part, l, u, v):
        s, c = coords(part, u, v)
        i, j = line_peers[l] * 2 + s, c * 2 + core
        arrived(chunk(i, j, part), recv_sem.at[i, j, part])

    def start_spread():
        if parts:
            own = pltpu.make_async_copy(gated_ref, out_ref.at[ch, ctx], own_sem.at[0])
            own.start()
            owns.append(own)
        for part, (first, rows) in enumerate(parts):
            mine = gated_ref.at[pl.ds(first, rows)]
            for s in range(1, lines):
                send(
                    line, side, column, part, mine, far_sem.at[part, s],
                    at(line_peers[s], side, column, core),
                )

    def cut(value):
        return jnp.concatenate([value[:, n * width : (n + 1) * width] for n in range(blocks)], axis=0)

    def glue(value):
        rows = value.shape[0] // blocks
        return jnp.concatenate([value[n * rows : (n + 1) * rows] for n in range(blocks)], axis=1)

    def dot(left, right, dims=((1,), (0,))):
        return lax.dot_general(
            left, right, (dims, ((), ())), precision=precise, preferred_element_type=jnp.float32
        )

    rows = gated_ref.shape[0]
    flat = ((1,), (1,))
    pass_cot(0)
    lag_spec[...] = dot(cut(dot(last_ref[...], two_ref[...]) * env_ref[...]), forward_ref[...])
    if lines > 1:
        send_half(1)
    for copy in seq_copies:
        copy.wait()
    if lines > 2:
        send_half(2)
    for n in range(3):
        filtered[n] = short_apply(seq[n].astype(jnp.float32), taps_ref[n])
    wide = (filtered[1] * filtered[2]).astype(jnp.bfloat16).astype(jnp.float32)
    product[...] = wide
    own_spec[...] = dot(cut(wide), forward_ref[...])

    def at_block(ref, n):
        return ref[n * rows : (n + 1) * rows]

    specs = [
        total(
            spectral_product(at_block(lag_spec, i), at_block(own_spec, k - i), width)
            for i in range(k + 1)
        )
        for k in range(blocks)
    ]
    double = dot(jnp.concatenate(specs, axis=0), inverse_ref[...])
    carry = jnp.concatenate(
        [jnp.zeros((rows, width), jnp.float32), double[: (blocks - 1) * rows, width:]], axis=0
    )
    value = glue(double[:, :width] + carry) + skip_ref[...] * product[...]
    long_out[...] = value
    gated_ref[...] = (filtered[0] * value).astype(gated_ref.dtype)

    start_spread()
    for l in range(lines):
        for part, (first, size) in enumerate(parts):
            if l:
                wait_for(part, l, 0, 0)
            pass_on(part, l, 0, 0, None if l else gated_ref.at[pl.ds(first, size)])
        if 2 < l + 3 < lines:
            send_half(l + 3)

    def second(l):
        for part in range(len(parts)):
            for u in range(1, sizes[part][0]):
                wait_for(part, l, u, 0)
                pass_on(part, l, u, 0, None)

    for s in range(1, columns):
        pass_cot(s)
    second(0)
    sums = finish_sum()
    for l in range(1, lines // 2):
        second(l)
    for copy in sums:
        copy.wait()

    cotangent = sum_ref[...].astype(jnp.float32)
    grad_long = (cotangent * filtered[0]).astype(jnp.bfloat16).astype(jnp.float32)
    stacked = cut(grad_long)
    after = jnp.concatenate([stacked[rows:], jnp.zeros((rows, width), jnp.float32)], axis=0)
    grad_spec = dot(jnp.concatenate([stacked, after], axis=1), inverse_ref[...], flat)

    def adjoint(ref):
        found = [
            total(
                spectral_adjoint(at_block(ref, k - j), grad_spec[k * rows : (k + 1) * rows], width)
                for k in range(j, blocks)
            )
            for j in range(blocks)
        ]
        return glue(dot(jnp.concatenate(found, axis=0), forward_ref[...], flat))

    grad_product = adjoint(lag_spec) + skip_ref[...] * grad_long
    grads = [cotangent * long_out[...], grad_product * filtered[2], grad_product * filtered[1]]
    for n in range(3):
        back_seq[n] = short_adjoint(grads[n], taps_ref[n]).astype(back_seq.dtype)
    backs = [
        remote(
            back_seq.at[:, :, span(ctx_peers[s])], back_out.at[:, ctx],
            back_send.at[0, s], back_recv.at[0, s], {"ctx": ctx_peers[s]},
        )
        for s in range(1, cycle)
    ]
    backs.append(
        pltpu.make_async_copy(back_seq.at[:, :, span(ctx)], back_out.at[:, ctx], own_sem.at[4])
    )
    backs[-1].start()
    for l in range(max(1, lines // 2), lines):
        second(l)

    grad_raw = adjoint(own_spec) * env_ref[...]
    last_own[...] = dot(grad_raw, two_ref[...], flat)
    slope = dot(last_flat_ref[...], grad_raw) * two_slope_ref[...]
    bands = features_ref.shape[0]
    small_own[bands:] = dot(one_ref[...], slope, flat)
    slope = dot(mid_ref[...], slope) * one_slope_ref[...]
    small_own[:bands] = dot(features_ref[...], slope, flat)
    smalls = []
    for s in range(1, cycle):
        to = {"ctx": ctx_peers[s]}
        smalls.append(
            remote(small_own, from_ctx.at[ctx], back_send.at[1, s], back_recv.at[1, s], to)
        )
        backs.append(
            remote(last_own, last_out.at[ctx], back_send.at[2, s], back_recv.at[2, s], to)
        )
    backs.append(pltpu.make_async_copy(last_own, last_out.at[ctx], own_sem.at[5]))
    backs[-1].start()
    from_ctx[ctx] = small_own[...]
    for copy in smalls:
        copy.wait()
    small_sum[...] = total(from_ctx[j] for j in range(cycle))
    smalls = [
        remote(small_sum, from_ch.at[ch], ch_send.at[s], ch_recv.at[s], {"ch": ch_peers[s]})
        for s in range(1, groups)
    ]
    for l in range(lines):
        for part in range(len(parts)):
            for u in range(sizes[part][0]):
                for v in range(1, sizes[part][1]):
                    wait_for(part, l, u, v)
                    pass_on(part, l, u, v, None)
    from_ch[ch] = small_sum[...]
    for copy in smalls:
        copy.wait()
    small_out[...] = total(from_ch[i] for i in range(groups))
    for copy in owns + backs:
        copy.wait()
    for s in range(columns):
        j = column_peers[s] * 2 + 1 - core
        arrived(cot_place(j), cot_recv.at[j])
    for part in range(len(parts)):
        for l in range(lines):
            for s in range(2):
                for c in range(columns):
                    i, j = line_peers[l] * 2 + side_peers[s], column_peers[c] * 2 + (1 - core)
                    arrived(chunk(i, j, part), recv_sem.at[i, j, part])
    for copy in pending:
        copy.wait_send()


def layer(ident, streams, terms, cot, taps, skip, env, last, mid, hidden, features, share):
    groups, cycle = lax.axis_size("ch"), lax.axis_size("ctx")
    _, channels, tokens = terms.shape
    rows, length = env.shape
    width = min(256, tokens)
    blocks = length // width
    lines, columns = groups // 2, cycle // 2
    cut = share // 16 * 13 // 16 * 16
    parts = [(0, cut), (cut, share - cut)] if 0 < cut < share else [(0, share)]
    if groups * cycle > 64:
        parts = []
    most = max(2, columns)
    count = max(1, len(parts))
    spread_shape = (groups, cycle, rows, length) if parts else (1, 1, 16, 128)
    units = last.shape[1]
    small = (features.shape[0] + mid.shape[0], units)
    dma, vmem = pltpu.SemaphoreType.DMA, pl.BlockSpec(memory_space=pltpu.VMEM)
    half, wide = jnp.bfloat16, jnp.float32
    forward, inverse = fourier_tables(width)
    gated, cot_all, spread, back, last_all, small_all = pl.pallas_call(
        functools.partial(layer_kernel, lines, columns, parts, tokens, share, width),
        out_shape=[
            jax.ShapeDtypeStruct((rows, length), half),
            jax.ShapeDtypeStruct((cot.shape[0], length), half),
            jax.ShapeDtypeStruct(spread_shape, half),
            jax.ShapeDtypeStruct((3, cycle, rows, tokens), half),
            jax.ShapeDtypeStruct((cycle,) + last.shape, wide),
            jax.ShapeDtypeStruct(small, wide),
        ],
        in_specs=in_any(1) + [vmem] + in_any(1) + [vmem] * 13,
        out_specs=[vmem] + in_any(4) + [vmem],
        scratch_shapes=[
            pltpu.VMEM((3, rows, length), half),
            pltpu.VMEM((3, rows, length), wide),
            pltpu.VMEM((rows, length), wide),
            pltpu.VMEM((rows, length), wide),
            pltpu.VMEM((blocks * rows, 2 * width), wide),
            pltpu.VMEM((blocks * rows, 2 * width), wide),
            pltpu.VMEM((rows, length), half),
            pltpu.VMEM((3, rows, length), half),
            pltpu.VMEM(last.shape, wide),
            pltpu.VMEM(small, wide),
            pltpu.VMEM((cycle,) + small, wide),
            pltpu.VMEM(small, wide),
            pltpu.VMEM((groups,) + small, wide),
            pltpu.VMEM((lines, channels, tokens), half),
            pltpu.VMEM((lines, channels, tokens), half),
            pltpu.VMEM((lines, channels, tokens), half),
            pltpu.VMEM((cycle, rows, tokens), half),
            dma((cycle,)),
            dma((cycle,)),
            dma((lines,)),
            dma((lines,)),
            dma((lines,)),
            dma((lines,)),
            dma((cycle,)),
            dma((cycle,)),
            dma((2, columns)),
            dma((cycle,)),
            dma((count, lines)),
            dma((count, lines, most)),
            dma((count, lines, most, most)),
            dma((count, lines, most, most)),
            dma((groups if parts else 1, cycle, count)),
            dma((6,)),
            dma((3, cycle)),
            dma((3, cycle)),
            dma((groups,)),
            dma((groups,)),
        ],
        compiler_params=pltpu.CompilerParams(
            collective_id=ident, has_side_effects=True, vmem_limit_bytes=56 * 2**20
        ),
    )(streams, terms, cot, taps, skip, env, last, last.T, mid, *hidden, features, forward, inverse)
    if not parts:
        spread = lax.all_gather(lax.all_gather(gated[:share], "ctx"), "ch")
    return cot_all, spread[:, :, :share], back[:, :, :share], last_all[:, :share], small_all


def band_features(bands, length):
    phases = 2.0 * math.pi / length * (np.arange(1, bands + 1)[:, None] * np.arange(length) % length)
    return np.concatenate([np.cos(phases), np.sin(phases)]).astype(np.float32)


def fourier_tables(width):
    double = 2 * width
    row, col = np.arange(width), np.arange(double)
    phase = 2.0 * math.pi / double * (row[:, None] * row[None, :] % double)
    forward_cos = np.cos(phase)
    forward_sin = np.where(row[None, :] == 0, (1 - 2 * (row % 2))[:, None], -np.sin(phase))
    phase = 2.0 * math.pi / double * (row[:, None] * col[None, :] % double)
    inverse_cos = np.where(row == 0, 1.0, 2.0)[:, None] / double * np.cos(phase)
    inverse_sin = np.where(
        row[:, None] == 0, (1 - 2 * (col % 2))[None, :] / double, -2.0 / double * np.sin(phase)
    )
    return (
        np.concatenate([forward_cos, forward_sin], axis=1).astype(np.float32),
        np.concatenate([inverse_cos, inverse_sin], axis=0).astype(np.float32),
    )


def spectral_product(left, right, width):
    lr, li = left[..., :width], left[..., width:]
    rr, ri = right[..., :width], right[..., width:]
    edge = lax.broadcasted_iota(jnp.int32, lr.shape, lr.ndim - 1) == 0
    cross = li * ri
    real = lr * rr - jnp.where(edge, 0.0, cross)
    imag = jnp.where(edge, cross, lr * ri + li * rr)
    return jnp.concatenate([real, imag], axis=-1)


def spectral_adjoint(left, right, width):
    lr, li = left[..., :width], left[..., width:]
    rr, ri = right[..., :width], right[..., width:]
    edge = lax.broadcasted_iota(jnp.int32, lr.shape, lr.ndim - 1) == 0
    cross = li * ri
    real = lr * rr + jnp.where(edge, 0.0, cross)
    imag = jnp.where(edge, cross, lr * ri - li * rr)
    return jnp.concatenate([real, imag], axis=-1)


def total(terms):
    terms = list(terms)
    value = terms[0]
    for term in terms[1:]:
        value = value + term
    return value


def short_apply(signal, taps):
    out = taps[:, 0:1] * signal
    for lag in range(1, taps.shape[1]):
        empty = jnp.zeros((signal.shape[0], lag), signal.dtype)
        out = out + taps[:, lag : lag + 1] * jnp.concatenate([empty, signal[:, :-lag]], axis=1)
    return out


def short_adjoint(signal, taps):
    out = taps[:, 0:1] * signal
    for lag in range(1, taps.shape[1]):
        empty = jnp.zeros((signal.shape[0], lag), signal.dtype)
        out = out + taps[:, lag : lag + 1] * jnp.concatenate([signal[:, lag:], empty], axis=1)
    return out


def shards(
    streams,
    short_taps,
    filter_in,
    filter_mid,
    filter_out,
    decay_rate,
    skip_gain,
    out_weight,
    grad_out,
):
    channels, tokens = streams.shape[1:]
    cycle, groups = lax.axis_size("ctx"), lax.axis_size("ch")
    ctx = lax.axis_index("ctx")
    length = tokens * cycle
    share = channels // cycle
    spare = -share % 16

    def padded(value, axis):
        pads = [(0, 0)] * value.ndim
        pads[axis] = (0, spare)
        return jnp.pad(value, pads) if spare else value

    def mine(value, axis):
        return padded(lax.dynamic_slice_in_dim(value, ctx * share, share, axis), axis)

    pieces = padded(streams.reshape(3, cycle, share, tokens), 2)
    terms = jnp.einsum("dc,dt->ct", out_weight, grad_out, preferred_element_type=jnp.float32)
    terms = terms.astype(jnp.bfloat16).reshape(groups, channels, tokens)
    features = band_features(filter_in.shape[0] // 2, length)
    before_one = jnp.einsum("fh,fs->hs", filter_in, features, precision=precise)
    one = jnp.sin(before_one)
    before_two = jnp.einsum("gh,gs->hs", filter_mid, one, precision=precise)
    hidden = [one, jnp.cos(before_one), jnp.sin(before_two), jnp.cos(before_two)]
    rate = mine(decay_rate, 0)[:, None]
    env = jnp.exp(-rate * jnp.arange(length).astype(jnp.float32)) * jnp.sqrt(rate)

    grad_all, gated, back, last, small = layer(
        0, pieces, terms, grad_out, mine(short_taps, 1), mine(skip_gain, 0)[:, None], env,
        mine(filter_out, 1).T, filter_mid, hidden, features, share,
    )
    gated = gated.reshape(groups * channels, length)
    here = lax.dynamic_slice_in_dim(gated, ctx * tokens, tokens, 1)
    layer_out = jnp.dot(out_weight, here, preferred_element_type=jnp.float32).astype(jnp.bfloat16)
    weight_grad = jnp.einsum("dt,ct->dc", grad_all, gated, preferred_element_type=jnp.float32)
    grad_filter_out = last.reshape(channels, filter_out.shape[0]).T
    cut = filter_in.shape[0]
    return (
        layer_out, back.reshape(streams.shape), small[:cut], small[cut:], grad_filter_out, weight_grad
    )


def solution(mesh):
    return jax.shard_map(
        shards,
        mesh=mesh,
        in_specs=(
            P(None, "ch", "ctx"),
            P(None, "ch", None),
            P(),
            P(),
            P(None, "ch"),
            P("ch"),
            P("ch"),
            P("ch", None),
            P("ch", "ctx"),
        ),
        out_specs=(P("ch", "ctx"), P(None, "ch", "ctx"), P(), P(), P(None, "ch"), P("ch", None)),
        check_vma=False,
    )
```
